32 devices in a mesh: chan: 8 (over z, x), ma: 4 (over y, core).
Axes of the slice: x: 2, y: 2, z: 4, core: 2. Of those that a mesh axis runs over, the one named last changes fastest.
Arguments:
- beam_table: bfloat16 [64, 1024, 2048], P(('ma', 'chan')), parts along dimension 0, may hold values from -0.125 to 0.125
- covariance: bfloat16 [8192, 16, 16], P(('ma', 'chan')), parts along dimension 0, as said below
- noise_var: float32 [64, 512], P(('ma', 'chan')), parts along dimension 0, may hold values from 0.5 to 4
- start_field: float32 [64, 512, 256], P(('ma', 'chan')), parts along dimension 0, may hold values from -4 to 4
- probes: float32 [64, 512, 256], P(('ma', 'chan')), parts along dimension 0, may hold values from -6 to 6
Outputs:
- solved: float32 [64, 512, 256], P(('ma', 'chan')), parts along dimension 0
- multipole_band_power: bfloat16 [8192, 16, 16], P(('ma', 'chan')), parts along dimension 0
The draws below stay inside these ranges and needn't reach their ends.
There are 4 independent parts, one for each index of `ma`. The reference program is written for one: setup_inputs(seed, part) draws one part's arguments, and reference() takes and returns one part's arrays. A program takes and returns all parts, laid end to end along the dimension named above; each array names one. Nothing has to cross between parts.
Inputs may be any that keep to these rules, and one draw needn't show every extreme that they name: Each covariance[l] is symmetric with diagonal entries between 1 and 2.
All inputs are finite; a program needn't handle non-finite values.
Results may differ from the reference program's by a relative error of at most 0.009.
Values may be sent and summed in bfloat16 or wider, within the bound.
A program may use at most 128 MiB of HBM per device.

```python
import math
import jax
import jax.numpy as jnp
from jax import lax

CHANNELS = 16
K = 512
L = 2048
PROBE_VECTOR_COUNT = 128
ITERS = 2


def draw_covariance(key, part):
    first_key = jax.random.fold_in(key, 11)
    second_key = jax.random.fold_in(key, 12)
    raw_values = jax.random.uniform(first_key, (L, CHANNELS, CHANNELS), jnp.float32, -1.0, 1.0)
    symmetric = 0.5 * (raw_values + jnp.swapaxes(raw_values, 1, 2))
    identity = jnp.eye(CHANNELS, dtype=jnp.float32)
    diagonal = 1.0 + jax.random.uniform(second_key, (L, CHANNELS, 1), jnp.float32)
    offdiag = (1.0 - identity) * (0.9 / math.sqrt(CHANNELS)) * symmetric
    return (identity * diagonal + offdiag).astype(jnp.bfloat16)


def block_scale(own_key, dims, split, smallest, largest):
    loudness, own = 1.0, jax.random.fold_in(own_key, 6)
    for position, parts in split:
        steps = jnp.exp(jax.random.uniform(jax.random.fold_in(own, position), (parts,), jnp.float32, smallest / len(split), largest / len(split)))
        loudness = loudness * jnp.repeat(steps, dims[position] // parts).reshape([-1 if axis == position else 1 for axis in range(len(dims))])
    return loudness


def scatter_about(own_key, dims, scale, bound, split=(), kind=jnp.bfloat16):
    values = jax.random.normal(own_key, dims, jnp.float32) * scale
    if len(split) > 0:
        values = block_scale(own_key, dims, split, -0.22, 0.18) * values
    return jnp.clip(values, min=-bound, max=bound).astype(kind)


def setup_inputs(seed: int = 0, part: int = 0) -> dict:
    streams_of = jax.random.split(jax.random.key(seed), 6)
    part_keys = jax.random.split(jax.random.fold_in(streams_of[5], part), 6)
    beam_table = scatter_about(part_keys[0], (CHANNELS, 2 * K, L), L ** -0.5, 0.125, ((0, 8),))
    covariance = draw_covariance(jax.random.fold_in(jax.random.fold_in(streams_of[5], part), 71), part)
    noise_var = jnp.clip(jnp.exp(math.log(4.0) - 2.0794415 * jax.random.uniform(part_keys[2], (CHANNELS, K), jnp.float32) ** block_scale(part_keys[2], (CHANNELS, K), ((0, 8),), -0.2, 0.2)), 0.5, 4.0)
    start_field = scatter_about(part_keys[3], (CHANNELS, K, 2 * PROBE_VECTOR_COUNT), 0.5, 4.0, ((0, 8),), jnp.float32)
    probes = scatter_about(part_keys[4], (CHANNELS, K, 2 * PROBE_VECTOR_COUNT), 1.0, 6.0, ((0, 8),), jnp.float32)
    return dict(beam_table=beam_table, covariance=covariance, noise_var=noise_var, start_field=start_field, probes=probes)


WEIGHT = 0.2


def project_back(beam_table, field_b):
    def one_channel(pair):
        table, values = pair
        reals = values[:, :PROBE_VECTOR_COUNT]
        imags = values[:, PROBE_VECTOR_COUNT:]
        lower = jnp.concatenate([imags, -reals], axis=1)
        stacked = jnp.concatenate([values, lower], axis=0)
        return jnp.dot(table.T, stacked, preferred_element_type=jnp.float32)
    return lax.map(one_channel, (beam_table, field_b))


def project_out(beam_table, channel_mixed):
    def one_channel(pair):
        table, values = pair
        product = jnp.dot(table, values, preferred_element_type=jnp.float32)
        upper = product[:K]
        lower = product[K:]
        return jnp.concatenate([upper[:, :PROBE_VECTOR_COUNT] - lower[:, PROBE_VECTOR_COUNT:], upper[:, PROBE_VECTOR_COUNT:] + lower[:, :PROBE_VECTOR_COUNT]], axis=1)
    return lax.map(one_channel, (beam_table, channel_mixed))


def reference(beam_table, covariance, noise_var, start_field, probes):
    field = start_field
    covariance_broad = covariance.astype(jnp.float32)
    for repeat in range(ITERS):
        field_b = field.astype(jnp.bfloat16)
        sky_map = project_back(beam_table, field_b).astype(jnp.bfloat16)
        channel_mixed = jnp.einsum('drj,jdi->rdi', covariance_broad, sky_map.astype(jnp.float32)).astype(jnp.bfloat16)
        image = project_out(beam_table, channel_mixed)
        field = field + WEIGHT * (probes - image - noise_var[:, :, None] * field)
    final_sky = project_back(beam_table, field.astype(jnp.bfloat16)).astype(jnp.bfloat16)
    broad_sky_map = final_sky.astype(jnp.float32)
    multipole_band_power = (jnp.einsum('mjk,ujk->jmu', broad_sky_map, broad_sky_map) / PROBE_VECTOR_COUNT).astype(jnp.bfloat16)
    return field, multipole_band_power
```

```python
import functools

import jax
import jax.numpy as jnp
from jax import lax
from jax.experimental import pallas as pl
from jax.experimental.pallas import tpu as pltpu
from jax.sharding import PartitionSpec as P

ITERS = 2


WEIGHT = 0.2

GROUP = 16
PIECES = 2


def kernel(
    beam_hbm, cov_ref, noise_ref, start_ref, probes_ref, solved_ref, power_ref,
    beam, beam_t, stacked, product, diag, sky, skies, mixed, back,
    load_sem, out_send, out_recv, back_send, back_recv,
):
    channels, modes, columns = start_ref.shape
    half = columns // 2
    owners = back.shape[2]
    rows = back.shape[4]
    owned = PIECES * rows
    groups = rows // GROUP
    block = GROUP * channels * owners
    me = lax.axis_index("chan")

    def partner(d):
        place = 0
        for bit in (4, 2, 1):
            mine = lax.rem(lax.div(me, bit), 2)
            flip = lax.rem(lax.div(jnp.int32(d), jnp.int32(bit)), jnp.int32(2))
            place = place + bit * (mine + flip - 2 * mine * flip)
        return place

    def load(d):
        cols = pl.ds(pl.multiple_of(partner(d) * owned, 128), owned)
        return pltpu.make_async_copy(
            beam_hbm.at[:, :, cols], beam.at[:, :, cols], load_sem.at[d]
        )

    def send_sky(it, s, d):
        return pltpu.make_async_remote_copy(
            src_ref=sky.at[s, d],
            dst_ref=skies.at[it, s, pl.ds(channels * me, channels)],
            send_sem=out_send.at[it, s, d],
            recv_sem=out_recv.at[it, s, d],
            device_id={"chan": partner(d)},
            device_id_type=pl.DeviceIdType.MESH,
        )

    def send_mixed(it, s, d):
        to = partner(d)
        return pltpu.make_async_remote_copy(
            src_ref=mixed.at[s, pl.ds(channels * to, channels)],
            dst_ref=back.at[it, s, me],
            send_sem=back_send.at[it, s, d],
            recv_sem=back_recv.at[it, s, d],
            device_id={"chan": to},
            device_id_type=pl.DeviceIdType.MESH,
        )

    def each(body):
        def step(i, carry):
            body(owners - 1 - i)
            return carry

        lax.fori_loop(0, owners - 1, step, 0)

    def start_load(d):
        load(d).start()

    each(start_load)
    load(0).start()

    barrier = pltpu.get_barrier_semaphore()

    def greet(d):
        pl.semaphore_signal(
            barrier, inc=1, device_id={"chan": partner(d)},
            device_id_type=pl.DeviceIdType.MESH,
        )

    each(greet)

    row = lax.broadcasted_iota(jnp.int32, (block, block), 0)
    col = lax.broadcasted_iota(jnp.int32, (block, block), 1)
    same = lax.rem(row, GROUP) == lax.rem(col, GROUP)
    width = cov_ref.shape[2]
    spread_row = lax.broadcasted_iota(jnp.int32, (width, block), 0)
    spread_col = lax.broadcasted_iota(jnp.int32, (width, block), 1)
    pick_row = lax.broadcasted_iota(jnp.int32, (block, width), 0)
    pick_col = lax.broadcasted_iota(jnp.int32, (block, width), 1)
    per_group = block // GROUP

    def stack(field):
        for ch in range(channels):
            values = field[ch].astype(jnp.bfloat16)
            stacked[ch, 0:modes, :] = values
            stacked[ch, modes : 2 * modes, 0:half] = values[:, half:]
            stacked[ch, modes : 2 * modes, half:] = -values[:, :half]

    def project(it, s, d, own):
        l0 = pl.multiple_of(partner(d) * owned + s * rows, 128)
        if it == 0 and s == 0:
            load(d).wait()
        for ch in range(channels):
            if it == 0:
                tile = beam[ch, :, pl.ds(l0, rows)].T
                beam_t[ch, pl.ds(l0, rows), :] = tile
            else:
                tile = beam_t[ch, pl.ds(l0, rows), :]
            value = jnp.dot(
                tile, stacked[ch], preferred_element_type=jnp.float32
            ).astype(jnp.bfloat16)
            if own:
                skies[it, s, channels * me + ch] = value
            else:
                sky[s, d, ch] = value

    def send_all(it):
        for s in range(PIECES):
            def step(d):
                project(it, s, d, False)
                send_sky(it, s, d).start()

            each(step)
        for s in range(PIECES):
            project(it, s, 0, True)

    def mix(it, s):
        def arrive(d):
            send_sky(it, s, d).wait_recv()

        each(arrive)

        def step(q, carry):
            r0 = pl.multiple_of(q * GROUP, GROUP)
            x = skies[it, s, :, pl.ds(r0, GROUP), :].reshape(block, columns)
            y = jnp.dot(diag[s, q], x, preferred_element_type=jnp.float32)
            mixed[s, :, pl.ds(r0, GROUP), :] = y.astype(jnp.bfloat16).reshape(
                per_group, GROUP, columns
            )
            return carry

        lax.fori_loop(0, groups, step, 0)

        def reply(d):
            send_mixed(it, s, d).start()

        each(reply)

    def add_image(it, s, d, own):
        owner = partner(d)
        l0 = pl.multiple_of(owner * owned + s * rows, 128)
        for ch in range(channels):
            if own:
                values = mixed[s, channels * me + ch]
            else:
                values = back[it, s, owner, ch]
            term = jnp.dot(
                beam[ch, :, pl.ds(l0, rows)], values,
                preferred_element_type=jnp.float32,
            )
            if own and s == 0:
                product[ch] = term
            else:
                product[ch] += term

    stack(start_ref)
    pl.semaphore_wait(barrier, owners - 1)

    for it in range(ITERS):
        send_all(it)
        if it == 0:
            for s in range(PIECES):
                def fill(q, carry):
                    spread = jnp.where(
                        spread_row == q * per_group + lax.div(spread_col, GROUP),
                        1.0, 0.0,
                    ).astype(jnp.bfloat16)
                    wide = jnp.dot(
                        cov_ref[s], spread, preferred_element_type=jnp.float32
                    )
                    diag[s, q] = jnp.where(same, wide, 0.0).astype(jnp.bfloat16)
                    return carry

                lax.fori_loop(0, groups, fill, 0)
        for s in range(PIECES):
            mix(it, s)
        for s in range(PIECES):
            add_image(it, s, 0, True)
        for s in range(PIECES):
            def collect(d):
                send_mixed(it, s, d).wait_recv()
                add_image(it, s, d, False)
                send_sky(it, s, d).wait_send()

            each(collect)
        for s in range(PIECES):
            def sent(d):
                send_mixed(it, s, d).wait_send()

            each(sent)
        field = start_ref if it == 0 else solved_ref
        for ch in range(channels):
            upper = product[ch, 0:modes, :]
            lower = product[ch, modes : 2 * modes, :]
            image = jnp.concatenate(
                [upper[:, :half] - lower[:, half:], upper[:, half:] + lower[:, :half]],
                axis=1,
            )
            old = field[ch]
            solved_ref[ch] = old + WEIGHT * (
                probes_ref[ch] - image - noise_ref[ch] * old
            )
        stack(solved_ref)

    send_all(ITERS)
    for s in range(PIECES):
        def arrive(d):
            send_sky(ITERS, s, d).wait_recv()

        each(arrive)

        def power(q, total):
            r0 = pl.multiple_of(q * GROUP, GROUP)
            x = skies[ITERS, s, :, pl.ds(r0, GROUP), :].reshape(block, columns)
            gram = lax.dot_general(
                x, x, (((1,), (1,)), ((), ())), preferred_element_type=jnp.float32
            )
            kept = jnp.where(same, gram / half, 0.0).astype(jnp.bfloat16)
            pick = jnp.where(
                pick_col == q * per_group + lax.div(pick_row, GROUP), 1.0, 0.0
            ).astype(jnp.bfloat16)
            return total + jnp.dot(kept, pick, preferred_element_type=jnp.float32)

        total = lax.fori_loop(
            0, groups, power, jnp.zeros((block, width), jnp.float32)
        )
        power_ref[s] = total.astype(jnp.bfloat16)
    for s in range(PIECES):
        def gone(d):
            send_sky(ITERS, s, d).wait_send()

        each(gone)


def fused(owners, beam_table, covariance, noise_var, start_field, probes):
    channels, modes, columns = start_field.shape
    owned, every, _ = covariance.shape
    rows = owned // PIECES
    groups = rows // GROUP
    block = GROUP * every
    cov = covariance.reshape(PIECES, groups, GROUP, every, every)
    cov = cov.transpose(0, 3, 2, 1, 4).reshape(PIECES, block, groups * every)
    vmem = pl.BlockSpec(memory_space=pltpu.VMEM)
    bf16 = jnp.bfloat16
    dma = pltpu.SemaphoreType.DMA
    solved, power = pl.pallas_call(
        kernel,
        out_shape=(
            jax.ShapeDtypeStruct(start_field.shape, jnp.float32),
            jax.ShapeDtypeStruct(cov.shape, bf16),
        ),
        in_specs=[pl.BlockSpec(memory_space=pl.ANY)] + [vmem] * 4,
        out_specs=(vmem, vmem),
        scratch_shapes=[
            pltpu.VMEM(beam_table.shape, bf16),
            pltpu.VMEM((channels, owned * owners, 2 * modes), bf16),
            pltpu.VMEM((channels, 2 * modes, columns), bf16),
            pltpu.VMEM((channels, 2 * modes, columns), jnp.float32),
            pltpu.VMEM((PIECES, groups, block, block), bf16),
            pltpu.VMEM((PIECES, owners, channels, rows, columns), bf16),
            pltpu.VMEM((ITERS + 1, PIECES, every, rows, columns), bf16),
            pltpu.VMEM((PIECES, every, rows, columns), bf16),
            pltpu.VMEM((ITERS, PIECES, owners, channels, rows, columns), bf16),
            dma((owners,)),
            dma((ITERS + 1, PIECES, owners)),
            dma((ITERS + 1, PIECES, owners)),
            dma((ITERS, PIECES, owners)),
            dma((ITERS, PIECES, owners)),
        ],
        compiler_params=pltpu.CompilerParams(
            collective_id=0, has_side_effects=True, vmem_limit_bytes=56 * 2**20
        ),
    )(beam_table, cov, noise_var[:, :, None], start_field, probes)
    power = power.reshape(PIECES, every, GROUP, groups, every)
    return solved, power.transpose(0, 3, 2, 1, 4).reshape(covariance.shape)


def project_back(beam_table, field_b):
    column_entries = field_b.shape[2] // 2
    reals = field_b[:, :, :column_entries]
    imags = field_b[:, :, column_entries:]
    lower = jnp.concatenate([imags, -reals], axis=2)
    stacked = jnp.concatenate([field_b, lower], axis=1)
    return jnp.einsum("fkl,fkc->flc", beam_table, stacked, preferred_element_type=jnp.float32)


def project_out(beam_table, mixed_back):
    column_entries = mixed_back.shape[2] // 2
    modes = beam_table.shape[1] // 2
    product = jnp.einsum("fkl,flc->fkc", beam_table, mixed_back, preferred_element_type=jnp.float32)
    upper = product[:, :modes]
    lower = product[:, modes:]
    return jnp.concatenate(
        [
            upper[:, :, :column_entries] - lower[:, :, column_entries:],
            upper[:, :, column_entries:] + lower[:, :, :column_entries],
        ],
        axis=2,
    )


def apply_operator(beam_table, covariance, field):
    field_b = field.astype(jnp.bfloat16)
    sky_map = project_back(beam_table, field_b).astype(jnp.bfloat16)
    channel_mixed = jnp.einsum(
        "drj,jdi->rdi",
        covariance,
        lax.all_to_all(sky_map, "chan", split_axis=1, concat_axis=0, tiled=True),
        preferred_element_type=jnp.float32,
    )
    mixed_back = lax.all_to_all(
        channel_mixed.astype(jnp.bfloat16), "chan", split_axis=0, concat_axis=1, tiled=True
    )
    return project_out(beam_table, mixed_back)


def fits(owners, beam_table, covariance):
    owned, every, _ = covariance.shape
    return (
        owners == 8
        and every * GROUP == 256
        and owned % (128 * PIECES) == 0
        and beam_table.size <= 4 * 2**20
    )


def on_device(owners, beam_table, covariance, noise_var, start_field, probes):
    if fits(owners, beam_table, covariance):
        return fused(owners, beam_table, covariance, noise_var, start_field, probes)
    field = start_field
    column_entries = field.shape[2] // 2
    for repeat in range(ITERS):
        image = apply_operator(beam_table, covariance, field)
        field = field + WEIGHT * (probes - image - noise_var[:, :, None] * field)
    final_sky = project_back(beam_table, field.astype(jnp.bfloat16)).astype(jnp.bfloat16)
    collected_parts = lax.all_to_all(final_sky, "chan", split_axis=1, concat_axis=0, tiled=True)
    multipole_band_power = (
        jnp.einsum(
            "mjk,ujk->jmu", collected_parts, collected_parts, preferred_element_type=jnp.float32
        )
        / column_entries
    )
    return (field, multipole_band_power.astype(jnp.bfloat16))


def solution(mesh):
    return jax.shard_map(
        functools.partial(on_device, mesh.shape["chan"]),
        mesh=mesh,
        in_specs=(
            P(("ma", "chan"), None, None),
            P(("ma", "chan"), None, None),
            P(("ma", "chan"), None),
            P(("ma", "chan"), None, None),
            P(("ma", "chan"), None, None),
        ),
        out_specs=(P(("ma", "chan"), None, None), P(("ma", "chan"), None, None)),
        check_vma=False,
    )
```

```python
import functools

import jax
import jax.numpy as jnp
from jax import lax
from jax.experimental import pallas as pl
from jax.experimental.pallas import tpu as pltpu
from jax.sharding import PartitionSpec as P

ITERS = 2


WEIGHT = 0.2

GROUP = 16
PIECES = 2


def kernel(
    beam_hbm, cov_ref, noise_ref, start_ref, probes_ref, solved_ref, power_ref,
    beam, beam_t, stacked, product, diag, sky, skies, mixed, back, noise,
    load_sem, out_send, out_recv, back_send, back_recv,
):
    channels, modes, columns = start_ref.shape
    half = columns // 2
    owners = back.shape[2]
    rows = back.shape[4]
    owned = PIECES * rows
    groups = rows // GROUP
    block = GROUP * channels * owners
    me = lax.axis_index("chan")

    def partner(d):
        place = 0
        for bit in (4, 2, 1):
            mine = lax.rem(lax.div(me, bit), 2)
            flip = lax.rem(lax.div(jnp.int32(d), jnp.int32(bit)), jnp.int32(2))
            place = place + bit * (mine + flip - 2 * mine * flip)
        return place

    def load(d):
        cols = pl.ds(pl.multiple_of(partner(d) * owned, 128), owned)
        return pltpu.make_async_copy(
            beam_hbm.at[:, :, cols], beam.at[:, :, cols], load_sem.at[d]
        )

    def send_sky(it, s, d):
        return pltpu.make_async_remote_copy(
            src_ref=sky.at[s, d],
            dst_ref=skies.at[it, s, pl.ds(channels * me, channels)],
            send_sem=out_send.at[it, s, d],
            recv_sem=out_recv.at[it, s, d],
            device_id={"chan": partner(d)},
            device_id_type=pl.DeviceIdType.MESH,
        )

    def send_mixed(it, s, d):
        to = partner(d)
        return pltpu.make_async_remote_copy(
            src_ref=mixed.at[s, pl.ds(channels * to, channels)],
            dst_ref=back.at[it, s, me],
            send_sem=back_send.at[it, s, d],
            recv_sem=back_recv.at[it, s, d],
            device_id={"chan": to},
            device_id_type=pl.DeviceIdType.MESH,
        )

    def each(body):
        def step(i, carry):
            body(owners - 1 - i)
            return carry

        lax.fori_loop(0, owners - 1, step, 0)

    def nearest(body):
        def step(i, carry):
            body(i + 1)
            return carry

        lax.fori_loop(0, owners - 1, step, 0)

    def start_load(d):
        load(d).start()

    each(start_load)
    load(0).start()

    barrier = pltpu.get_barrier_semaphore()

    def greet(d):
        pl.semaphore_signal(
            barrier, inc=1, device_id={"chan": partner(d)},
            device_id_type=pl.DeviceIdType.MESH,
        )

    each(greet)

    row = lax.broadcasted_iota(jnp.int32, (block, block), 0)
    col = lax.broadcasted_iota(jnp.int32, (block, block), 1)
    same = lax.rem(row, GROUP) == lax.rem(col, GROUP)
    across = lax.rem(row, GROUP) == lax.div(col, GROUP)
    alike = jnp.where(lax.div(row, GROUP) == lax.div(col, GROUP), 1.0, 0.0).astype(
        jnp.bfloat16
    )
    spot_row = lax.broadcasted_iota(jnp.int32, (owned, block), 0)
    spot_col = lax.broadcasted_iota(jnp.int32, (owned, block), 1)
    place_row = lax.broadcasted_iota(jnp.int32, (block, owned), 0)
    place_col = lax.broadcasted_iota(jnp.int32, (block, owned), 1)
    per_group = block // GROUP

    def stack(field):
        for ch in range(channels):
            values = field[ch].astype(jnp.bfloat16)
            stacked[ch, 0:modes, :] = values
            stacked[ch, modes : 2 * modes, 0:half] = values[:, half:]
            stacked[ch, modes : 2 * modes, half:] = -values[:, :half]

    def project(it, s, d, own):
        l0 = pl.multiple_of(partner(d) * owned + s * rows, 128)
        if it == 0 and s == 0:
            load(d).wait()
        for ch in range(channels):
            if it == 0:
                tile = beam[ch, :, pl.ds(l0, rows)].T
                beam_t[ch, pl.ds(l0, rows), :] = tile
            else:
                tile = beam_t[ch, pl.ds(l0, rows), :]
            value = jnp.dot(
                tile, stacked[ch], preferred_element_type=jnp.float32
            ).astype(jnp.bfloat16)
            if own:
                skies[it, s, channels * me + ch] = value
            else:
                sky[s, d, ch] = value

    def send_all(it):
        for s in range(PIECES):
            def step(d):
                project(it, s, d, False)
                send_sky(it, s, d).start()

            each(step)
        for s in range(PIECES):
            project(it, s, 0, True)

    def fill(s):
        table = cov_ref[...].reshape(block, owned)

        def step(q, carry):
            base = s * rows + q * GROUP
            spot = jnp.where(
                spot_row == base + lax.rem(spot_col, GROUP), 1.0, 0.0
            ).astype(jnp.bfloat16)
            wide = jnp.dot(table, spot, preferred_element_type=jnp.float32)
            wide = jnp.where(across, wide, 0.0).astype(jnp.bfloat16)
            wide = jnp.dot(alike, wide, preferred_element_type=jnp.float32)
            diag[s, q] = jnp.where(same, wide, 0.0).astype(jnp.bfloat16)
            return carry

        lax.fori_loop(0, groups, step, 0, unroll=2)

    def mix(it, s):
        def arrive(d):
            send_sky(it, s, d).wait_recv()

        each(arrive)

        def step(q, carry):
            r0 = pl.multiple_of(q * GROUP, GROUP)
            x = skies[it, s, :, pl.ds(r0, GROUP), :].reshape(block, columns)
            y = jnp.dot(diag[s, q], x, preferred_element_type=jnp.float32)
            mixed[s, :, pl.ds(r0, GROUP), :] = y.astype(jnp.bfloat16).reshape(
                per_group, GROUP, columns
            )
            return carry

        lax.fori_loop(0, groups, step, 0, unroll=True)

        def reply(d):
            send_mixed(it, s, d).start()

        each(reply)

    def add_image(it, s, d, own):
        owner = partner(d)
        l0 = pl.multiple_of(owner * owned + s * rows, 128)
        for ch in range(channels):
            if own:
                values = mixed[s, channels * me + ch]
            else:
                values = back[it, s, owner, ch]
            term = jnp.dot(
                beam[ch, :, pl.ds(l0, rows)], values,
                preferred_element_type=jnp.float32,
            )
            if own and s == 0:
                product[ch] = term
            else:
                product[ch] += term

    stack(start_ref)
    pl.semaphore_wait(barrier, owners - 1)

    for it in range(ITERS):
        send_all(it)
        if it == 0:
            for ch in range(channels):
                noise[ch] = jnp.broadcast_to(
                    noise_ref[ch : ch + 1, :], (half, modes)
                ).T
        for s in range(PIECES):
            if it == 0:
                fill(s)
            mix(it, s)
        for s in range(PIECES):
            add_image(it, s, 0, True)
        for s in range(PIECES):
            def collect(d):
                send_mixed(it, s, d).wait_recv()
                add_image(it, s, d, False)
                send_sky(it, s, d).wait_send()

            nearest(collect)
        for s in range(PIECES):
            def sent(d):
                send_mixed(it, s, d).wait_send()

            each(sent)
        field = start_ref if it == 0 else solved_ref
        for ch in range(channels):
            upper = product[ch, 0:modes, :]
            lower = product[ch, modes : 2 * modes, :]
            image = jnp.concatenate(
                [upper[:, :half] - lower[:, half:], upper[:, half:] + lower[:, :half]],
                axis=1,
            )
            old = field[ch]
            solved_ref[ch] = old + WEIGHT * (
                probes_ref[ch] - image - jnp.concatenate([noise[ch], noise[ch]], axis=1) * old
            )
        stack(solved_ref)

    send_all(ITERS)
    total = jnp.zeros((block, owned), jnp.float32)
    for s in range(PIECES):
        def arrive(d):
            send_sky(ITERS, s, d).wait_recv()

        each(arrive)

        def power(q, total):
            r0 = pl.multiple_of(q * GROUP, GROUP)
            x = skies[ITERS, s, :, pl.ds(r0, GROUP), :].reshape(block, columns)
            gram = lax.dot_general(
                x, x, (((1,), (1,)), ((), ())), preferred_element_type=jnp.float32
            )
            kept = jnp.where(same, gram / half, 0.0).astype(jnp.bfloat16)
            kept = jnp.dot(alike, kept, preferred_element_type=jnp.float32)
            kept = jnp.where(across, kept, 0.0).astype(jnp.bfloat16)
            place = jnp.where(
                place_col == s * rows + q * GROUP + lax.rem(place_row, GROUP), 1.0, 0.0
            ).astype(jnp.bfloat16)
            return total + jnp.dot(kept, place, preferred_element_type=jnp.float32)

        total = lax.fori_loop(0, groups, power, total, unroll=True)
    power_ref[...] = total.astype(jnp.bfloat16).reshape(power_ref.shape)
    for s in range(PIECES):
        def gone(d):
            send_sky(ITERS, s, d).wait_send()

        each(gone)


def fused(owners, beam_table, covariance, noise_var, start_field, probes):
    channels, modes, columns = start_field.shape
    owned, every, _ = covariance.shape
    rows = owned // PIECES
    groups = rows // GROUP
    block = GROUP * every
    cov = covariance.transpose(1, 2, 0)
    vmem = pl.BlockSpec(memory_space=pltpu.VMEM)
    bf16 = jnp.bfloat16
    dma = pltpu.SemaphoreType.DMA
    solved, power = pl.pallas_call(
        kernel,
        out_shape=(
            jax.ShapeDtypeStruct(start_field.shape, jnp.float32),
            jax.ShapeDtypeStruct(cov.shape, bf16),
        ),
        in_specs=[pl.BlockSpec(memory_space=pl.ANY)] + [vmem] * 4,
        out_specs=(vmem, vmem),
        scratch_shapes=[
            pltpu.VMEM(beam_table.shape, bf16),
            pltpu.VMEM((channels, owned * owners, 2 * modes), bf16),
            pltpu.VMEM((channels, 2 * modes, columns), bf16),
            pltpu.VMEM((channels, 2 * modes, columns), jnp.float32),
            pltpu.VMEM((PIECES, groups, block, block), bf16),
            pltpu.VMEM((PIECES, owners, channels, rows, columns), bf16),
            pltpu.VMEM((ITERS + 1, PIECES, every, rows, columns), bf16),
            pltpu.VMEM((PIECES, every, rows, columns), bf16),
            pltpu.VMEM((ITERS, PIECES, owners, channels, rows, columns), bf16),
            pltpu.VMEM((channels, modes, columns // 2), jnp.float32),
            dma((owners,)),
            dma((ITERS + 1, PIECES, owners)),
            dma((ITERS + 1, PIECES, owners)),
            dma((ITERS, PIECES, owners)),
            dma((ITERS, PIECES, owners)),
        ],
        compiler_params=pltpu.CompilerParams(
            collective_id=0, has_side_effects=True, vmem_limit_bytes=56 * 2**20
        ),
    )(beam_table, cov, noise_var, start_field, probes)
    return solved, power.transpose(2, 0, 1)


def project_back(beam_table, field_b):
    column_entries = field_b.shape[2] // 2
    reals = field_b[:, :, :column_entries]
    imags = field_b[:, :, column_entries:]
    lower = jnp.concatenate([imags, -reals], axis=2)
    stacked = jnp.concatenate([field_b, lower], axis=1)
    return jnp.einsum("fkl,fkc->flc", beam_table, stacked, preferred_element_type=jnp.float32)


def project_out(beam_table, mixed_back):
    column_entries = mixed_back.shape[2] // 2
    modes = beam_table.shape[1] // 2
    product = jnp.einsum("fkl,flc->fkc", beam_table, mixed_back, preferred_element_type=jnp.float32)
    upper = product[:, :modes]
    lower = product[:, modes:]
    return jnp.concatenate(
        [
            upper[:, :, :column_entries] - lower[:, :, column_entries:],
            upper[:, :, column_entries:] + lower[:, :, :column_entries],
        ],
        axis=2,
    )


def apply_operator(beam_table, covariance, field):
    field_b = field.astype(jnp.bfloat16)
    sky_map = project_back(beam_table, field_b).astype(jnp.bfloat16)
    channel_mixed = jnp.einsum(
        "drj,jdi->rdi",
        covariance,
        lax.all_to_all(sky_map, "chan", split_axis=1, concat_axis=0, tiled=True),
        preferred_element_type=jnp.float32,
    )
    mixed_back = lax.all_to_all(
        channel_mixed.astype(jnp.bfloat16), "chan", split_axis=0, concat_axis=1, tiled=True
    )
    return project_out(beam_table, mixed_back)


def fits(owners, beam_table, covariance):
    owned, every, _ = covariance.shape
    return (
        owners == 8
        and every * GROUP == 256
        and owned % (128 * PIECES) == 0
        and beam_table.size <= 4 * 2**20
    )


def on_device(owners, beam_table, covariance, noise_var, start_field, probes):
    if fits(owners, beam_table, covariance):
        return fused(owners, beam_table, covariance, noise_var, start_field, probes)
    field = start_field
    column_entries = field.shape[2] // 2
    for repeat in range(ITERS):
        image = apply_operator(beam_table, covariance, field)
        field = field + WEIGHT * (probes - image - noise_var[:, :, None] * field)
    final_sky = project_back(beam_table, field.astype(jnp.bfloat16)).astype(jnp.bfloat16)
    collected_parts = lax.all_to_all(final_sky, "chan", split_axis=1, concat_axis=0, tiled=True)
    multipole_band_power = (
        jnp.einsum(
            "mjk,ujk->jmu", collected_parts, collected_parts, preferred_element_type=jnp.float32
        )
        / column_entries
    )
    return (field, multipole_band_power.astype(jnp.bfloat16))


def solution(mesh):
    return jax.shard_map(
        functools.partial(on_device, mesh.shape["chan"]),
        mesh=mesh,
        in_specs=(
            P(("ma", "chan"), None, None),
            P(("ma", "chan"), None, None),
            P(("ma", "chan"), None),
            P(("ma", "chan"), None, None),
            P(("ma", "chan"), None, None),
        ),
        out_specs=(P(("ma", "chan"), None, None), P(("ma", "chan"), None, None)),
        check_vma=False,
    )
```

```python
import functools

import jax
import jax.numpy as jnp
from jax import lax
from jax.experimental import pallas as pl
from jax.experimental.pallas import tpu as pltpu
from jax.sharding import PartitionSpec as P

ITERS = 2


WEIGHT = 0.2

GROUP = 16
PIECES = 2


def kernel(
    beam_hbm, cov_ref, noise_ref, start_ref, probes_ref, solved_ref, power_ref,
    beam, beam_t, stacked, product, diag, sky, skies, mixed, back, noise,
    load_sem, out_send, out_recv, back_send, back_recv,
):
    channels, modes, columns = start_ref.shape
    half = columns // 2
    owners = back.shape[2]
    rows = back.shape[4]
    owned = PIECES * rows
    groups = rows // GROUP
    block = GROUP * channels * owners
    me = lax.axis_index("chan")

    def partner(d):
        place = 0
        for bit in (4, 2, 1):
            mine = lax.rem(lax.div(me, bit), 2)
            flip = lax.rem(lax.div(jnp.int32(d), jnp.int32(bit)), jnp.int32(2))
            place = place + bit * (mine + flip - 2 * mine * flip)
        return place

    def load(d):
        cols = pl.ds(pl.multiple_of(partner(d) * owned, 128), owned)
        return pltpu.make_async_copy(
            beam_hbm.at[:, :, cols], beam.at[:, :, cols], load_sem.at[d]
        )

    def send_sky(it, s, d):
        return pltpu.make_async_remote_copy(
            src_ref=sky.at[s, d],
            dst_ref=skies.at[it, s, pl.ds(channels * me, channels)],
            send_sem=out_send.at[it, s, d],
            recv_sem=out_recv.at[it, s, d],
            device_id={"chan": partner(d)},
            device_id_type=pl.DeviceIdType.MESH,
        )

    def send_mixed(it, s, d):
        to = partner(d)
        return pltpu.make_async_remote_copy(
            src_ref=mixed.at[s, pl.ds(channels * to, channels)],
            dst_ref=back.at[it, s, me],
            send_sem=back_send.at[it, s, d],
            recv_sem=back_recv.at[it, s, d],
            device_id={"chan": to},
            device_id_type=pl.DeviceIdType.MESH,
        )

    def each(body):
        def step(i, carry):
            body(owners - 1 - i)
            return carry

        lax.fori_loop(0, owners - 1, step, 0)

    def nearest(body):
        def step(i, carry):
            body(i + 1)
            return carry

        lax.fori_loop(0, owners - 1, step, 0)

    def start_load(d):
        load(d).start()

    each(start_load)
    load(0).start()

    barrier = pltpu.get_barrier_semaphore()

    def greet(d):
        pl.semaphore_signal(
            barrier, inc=1, device_id={"chan": partner(d)},
            device_id_type=pl.DeviceIdType.MESH,
        )

    each(greet)

    row = lax.broadcasted_iota(jnp.int32, (block, block), 0)
    col = lax.broadcasted_iota(jnp.int32, (block, block), 1)
    same = lax.rem(row, GROUP) == lax.rem(col, GROUP)
    across = lax.rem(row, GROUP) == lax.div(col, GROUP)
    alike = jnp.where(lax.div(row, GROUP) == lax.div(col, GROUP), 1.0, 0.0).astype(
        jnp.bfloat16
    )
    spot_row = lax.broadcasted_iota(jnp.int32, (owned, block), 0)
    spot_col = lax.broadcasted_iota(jnp.int32, (owned, block), 1)
    place_row = lax.broadcasted_iota(jnp.int32, (block, owned), 0)
    place_col = lax.broadcasted_iota(jnp.int32, (block, owned), 1)
    per_group = block // GROUP

    def stack(field):
        for ch in range(channels):
            values = field[ch].astype(jnp.bfloat16)
            stacked[ch, 0:modes, :] = values
            stacked[ch, modes : 2 * modes, 0:half] = values[:, half:]
            stacked[ch, modes : 2 * modes, half:] = -values[:, :half]

    def project(it, s, d, own):
        l0 = pl.multiple_of(partner(d) * owned + s * rows, 128)
        if it == 0 and s == 0:
            load(d).wait()
        for ch in range(channels):
            if it == 0:
                tile = beam[ch, :, pl.ds(l0, rows)].T
                beam_t[ch, pl.ds(l0, rows), :] = tile
            else:
                tile = beam_t[ch, pl.ds(l0, rows), :]
            value = jnp.dot(
                tile, stacked[ch], preferred_element_type=jnp.float32
            ).astype(jnp.bfloat16)
            if own:
                skies[it, s, channels * me + ch] = value
            else:
                sky[s, d, ch] = value

    def send_all(it):
        for s in range(PIECES):
            def step(d):
                project(it, s, d, False)
                send_sky(it, s, d).start()

            each(step)
        for s in range(PIECES):
            project(it, s, 0, True)

    def fill(s):
        table = cov_ref[...].reshape(block, owned)

        def step(q, carry):
            base = s * rows + q * GROUP
            spot = jnp.where(
                spot_row == base + lax.rem(spot_col, GROUP), 1.0, 0.0
            ).astype(jnp.bfloat16)
            wide = jnp.dot(table, spot, preferred_element_type=jnp.float32)
            wide = jnp.where(across, wide, 0.0).astype(jnp.bfloat16)
            wide = jnp.dot(alike, wide, preferred_element_type=jnp.float32)
            diag[s, q] = jnp.where(same, wide, 0.0).astype(jnp.bfloat16)
            return carry

        lax.fori_loop(0, groups, step, 0, unroll=2)

    def mix(it, s):
        def arrive(d):
            send_sky(it, s, d).wait_recv()

        each(arrive)

        def step(q, carry):
            r0 = pl.multiple_of(q * GROUP, GROUP)
            x = skies[it, s, :, pl.ds(r0, GROUP), :].reshape(block, columns)
            y = jnp.dot(diag[s, q], x, preferred_element_type=jnp.float32)
            mixed[s, :, pl.ds(r0, GROUP), :] = y.astype(jnp.bfloat16).reshape(
                per_group, GROUP, columns
            )
            return carry

        lax.fori_loop(0, groups, step, 0, unroll=True)

        def reply(d):
            send_mixed(it, s, d).start()

        each(reply)

    def add_image(it, s, d, own):
        owner = partner(d)
        l0 = pl.multiple_of(owner * owned + s * rows, 128)
        for ch in range(channels):
            if own:
                values = mixed[s, channels * me + ch]
            else:
                values = back[it, s, owner, ch]
            term = jnp.dot(
                beam[ch, :, pl.ds(l0, rows)], values,
                preferred_element_type=jnp.float32,
            )
            if own and s == 0:
                product[ch] = term
            else:
                product[ch] += term

    stack(start_ref)
    pl.semaphore_wait(barrier, owners - 1)

    for it in range(ITERS):
        send_all(it)
        if it == 0:
            for ch in range(channels):
                noise[ch] = jnp.broadcast_to(
                    noise_ref[ch : ch + 1, :], (half, modes)
                ).T
        for s in range(PIECES):
            if it == 0:
                fill(s)
            mix(it, s)
        for s in range(PIECES):
            add_image(it, s, 0, True)
        for s in range(PIECES):
            def collect(d):
                send_mixed(it, s, d).wait_recv()
                add_image(it, s, d, False)
                send_sky(it, s, d).wait_send()

            nearest(collect)
        for s in range(PIECES):
            def sent(d):
                send_mixed(it, s, d).wait_send()

            each(sent)
        field = start_ref if it == 0 else solved_ref
        for ch in range(channels):
            upper = product[ch, 0:modes, :]
            lower = product[ch, modes : 2 * modes, :]
            image = jnp.concatenate(
                [upper[:, :half] - lower[:, half:], upper[:, half:] + lower[:, :half]],
                axis=1,
            )
            old = field[ch]
            solved_ref[ch] = old + WEIGHT * (
                probes_ref[ch] - image - jnp.concatenate([noise[ch], noise[ch]], axis=1) * old
            )
        stack(solved_ref)

    send_all(ITERS)
    total = jnp.zeros((block, owned), jnp.float32)
    for s in range(PIECES):
        def arrive(d):
            send_sky(ITERS, s, d).wait_recv()

        each(arrive)

        def power(q, total):
            r0 = pl.multiple_of(q * GROUP, GROUP)
            x = skies[ITERS, s, :, pl.ds(r0, GROUP), :].reshape(block, columns)
            gram = lax.dot_general(
                x, x, (((1,), (1,)), ((), ())), preferred_element_type=jnp.float32
            )
            kept = jnp.where(same, gram / half, 0.0).astype(jnp.bfloat16)
            kept = jnp.dot(alike, kept, preferred_element_type=jnp.float32)
            kept = jnp.where(across, kept, 0.0).astype(jnp.bfloat16)
            place = jnp.where(
                place_col == s * rows + q * GROUP + lax.rem(place_row, GROUP), 1.0, 0.0
            ).astype(jnp.bfloat16)
            return total + jnp.dot(kept, place, preferred_element_type=jnp.float32)

        total = lax.fori_loop(0, groups, power, total, unroll=True)
    power_ref[...] = total.astype(jnp.bfloat16).reshape(power_ref.shape)
    for s in range(PIECES):
        def gone(d):
            send_sky(ITERS, s, d).wait_send()

        each(gone)


def hand_over(solved_ref, power_ref, solved_out, power_out):
    solved_out[...] = solved_ref[...]
    power_out[...] = power_ref[...]


def fused(owners, beam_table, covariance, noise_var, start_field, probes):
    channels, modes, columns = start_field.shape
    owned, every, _ = covariance.shape
    rows = owned // PIECES
    groups = rows // GROUP
    block = GROUP * every
    cov = covariance.transpose(1, 2, 0)
    vmem = pl.BlockSpec(memory_space=pltpu.VMEM)
    bf16 = jnp.bfloat16
    dma = pltpu.SemaphoreType.DMA
    solved, power = pl.pallas_call(
        kernel,
        out_shape=(
            jax.ShapeDtypeStruct(start_field.shape, jnp.float32),
            jax.ShapeDtypeStruct(cov.shape, bf16),
        ),
        in_specs=[pl.BlockSpec(memory_space=pl.ANY)] + [vmem] * 4,
        out_specs=(vmem, vmem),
        scratch_shapes=[
            pltpu.VMEM(beam_table.shape, bf16),
            pltpu.VMEM((channels, owned * owners, 2 * modes), bf16),
            pltpu.VMEM((channels, 2 * modes, columns), bf16),
            pltpu.VMEM((channels, 2 * modes, columns), jnp.float32),
            pltpu.VMEM((PIECES, groups, block, block), bf16),
            pltpu.VMEM((PIECES, owners, channels, rows, columns), bf16),
            pltpu.VMEM((ITERS + 1, PIECES, every, rows, columns), bf16),
            pltpu.VMEM((PIECES, every, rows, columns), bf16),
            pltpu.VMEM((ITERS, PIECES, owners, channels, rows, columns), bf16),
            pltpu.VMEM((channels, modes, columns // 2), jnp.float32),
            dma((owners,)),
            dma((ITERS + 1, PIECES, owners)),
            dma((ITERS + 1, PIECES, owners)),
            dma((ITERS, PIECES, owners)),
            dma((ITERS, PIECES, owners)),
        ],
        compiler_params=pltpu.CompilerParams(
            collective_id=0, has_side_effects=True, vmem_limit_bytes=56 * 2**20
        ),
    )(beam_table, cov, noise_var, start_field, probes)
    solved, power = pl.pallas_call(
        hand_over,
        out_shape=(
            jax.ShapeDtypeStruct(solved.shape, solved.dtype),
            jax.ShapeDtypeStruct(power.shape, power.dtype),
        ),
        in_specs=[vmem] * 2,
        out_specs=(vmem, vmem),
    )(solved, power)
    return solved, power.transpose(2, 0, 1)


def project_back(beam_table, field_b):
    column_entries = field_b.shape[2] // 2
    reals = field_b[:, :, :column_entries]
    imags = field_b[:, :, column_entries:]
    lower = jnp.concatenate([imags, -reals], axis=2)
    stacked = jnp.concatenate([field_b, lower], axis=1)
    return jnp.einsum("fkl,fkc->flc", beam_table, stacked, preferred_element_type=jnp.float32)


def project_out(beam_table, mixed_back):
    column_entries = mixed_back.shape[2] // 2
    modes = beam_table.shape[1] // 2
    product = jnp.einsum("fkl,flc->fkc", beam_table, mixed_back, preferred_element_type=jnp.float32)
    upper = product[:, :modes]
    lower = product[:, modes:]
    return jnp.concatenate(
        [
            upper[:, :, :column_entries] - lower[:, :, column_entries:],
            upper[:, :, column_entries:] + lower[:, :, :column_entries],
        ],
        axis=2,
    )


def apply_operator(beam_table, covariance, field):
    field_b = field.astype(jnp.bfloat16)
    sky_map = project_back(beam_table, field_b).astype(jnp.bfloat16)
    channel_mixed = jnp.einsum(
        "drj,jdi->rdi",
        covariance,
        lax.all_to_all(sky_map, "chan", split_axis=1, concat_axis=0, tiled=True),
        preferred_element_type=jnp.float32,
    )
    mixed_back = lax.all_to_all(
        channel_mixed.astype(jnp.bfloat16), "chan", split_axis=0, concat_axis=1, tiled=True
    )
    return project_out(beam_table, mixed_back)


def fits(owners, beam_table, covariance):
    owned, every, _ = covariance.shape
    return (
        owners == 8
        and every * GROUP == 256
        and owned % (128 * PIECES) == 0
        and beam_table.size <= 4 * 2**20
    )


def on_device(owners, beam_table, covariance, noise_var, start_field, probes):
    if fits(owners, beam_table, covariance):
        return fused(owners, beam_table, covariance, noise_var, start_field, probes)
    field = start_field
    column_entries = field.shape[2] // 2
    for repeat in range(ITERS):
        image = apply_operator(beam_table, covariance, field)
        field = field + WEIGHT * (probes - image - noise_var[:, :, None] * field)
    final_sky = project_back(beam_table, field.astype(jnp.bfloat16)).astype(jnp.bfloat16)
    collected_parts = lax.all_to_all(final_sky, "chan", split_axis=1, concat_axis=0, tiled=True)
    multipole_band_power = (
        jnp.einsum(
            "mjk,ujk->jmu", collected_parts, collected_parts, preferred_element_type=jnp.float32
        )
        / column_entries
    )
    return (field, multipole_band_power.astype(jnp.bfloat16))


def solution(mesh):
    return jax.shard_map(
        functools.partial(on_device, mesh.shape["chan"]),
        mesh=mesh,
        in_specs=(
            P(("ma", "chan"), None, None),
            P(("ma", "chan"), None, None),
            P(("ma", "chan"), None),
            P(("ma", "chan"), None, None),
            P(("ma", "chan"), None, None),
        ),
        out_specs=(P(("ma", "chan"), None, None), P(("ma", "chan"), None, None)),
        check_vma=False,
    )
```
